256 devices in a mesh: gi: 16 (over y, x), gj: 8 (over z_hi, core), ch: 2 (over z_lo).
Axes of the slice: x: 4, y: 4, z: 8 (z_hi: 4, z_lo: 2; z = z_hi * 2 + z_lo), core: 2. Of those that a mesh axis runs over, the one named last changes fastest.
Arguments:
- samples: bfloat16 [4096, 512, 32], P(('gi', 'gj'), 'ch'), may hold values from -6 to 6
- destination: int32 [1048576, 1], P(('gi', 'gj', 'ch')), may hold values from 0 to 127; in each aligned block of 4096 rows (0 to 4095, 4096 to 8191, ...) at most 64 rows name the same one
- offset: int32 [1048576], P(('gi', 'gj', 'ch')), may hold values from 0 to 511
- weight: bfloat16 [1048576], P(('gi', 'gj', 'ch')), may hold values from 0.25 to 4
Outputs:
- grid_tiles: float32 [2, 128, 512, 512], P('ch', ('gi', 'gj'))
The draws below stay inside these ranges and needn't reach their ends.
Inputs may be any that keep to these rules, and one draw needn't show every extreme that they name: `destination`: the 4096 rows of one device name one tile at most 64 times, and exactly 64 times for some tile of some device.
All inputs are finite; a program needn't handle non-finite values.
Results may differ from the reference program's by a relative error of at most 0.0048.
Values may be sent and summed in bfloat16 or wider, within the bound.
No kernel may reach another device: no remote copies, remote signals or barrier semaphores. Data moves between devices by JAX's collectives and lax.ppermute only.
A program may use at most 128 MiB of HBM per device.

```python
import math
import jax
import jax.numpy as jnp
import numpy as np
from jax import lax

N_IN = 4096
NCHAN = 16
TAPS = 32
TV = 256
SPEC = 512
CHAN_DEV = 8
IN_DEV = 32
ROWG = 256
COLG = 512
R_DEV = 4096
CAP = 64
TU = 512
ROWS_ALL = 1048576
N_GI = 16
N_GJ = 8
N_CH = 2


def plant(array, own_key, low, high):
    index_at = [jax.random.randint(jax.random.fold_in(own_key, axis), (), 0, length) for axis, length in enumerate(array.shape)]
    widest = array.shape.index(max(array.shape))
    next_to = index_at[:widest] + [(index_at[widest] + 1) % array.shape[widest]] + index_at[widest + 1:]
    return array.at[tuple(index_at)].set(low).at[tuple(next_to)].set(high)


def levels(rng, shape, split, least, top_value):
    gain = 1.0
    for dim, shards_of in split:
        draws = jax.random.uniform(jax.random.fold_in(jax.random.fold_in(rng, 6), dim), (shards_of,), jnp.float32, least / len(split), top_value / len(split))
        gain = gain * jnp.repeat(jnp.exp(draws), shape[dim] // shards_of).reshape((-1,) + (1,) * (len(shape) - 1 - dim))
    return gain


def deal_out(key, own, number, rows, amount, top, limit, slope):
    ranking = jax.random.permutation(key, amount)
    packed, usual = load_shares(amount, rows * top, limit, slope, True), load_shares(amount, rows * top, limit, slope, False)
    places = jnp.arange(amount)

    def named(sizes, offset_by):
        used = int((sizes > 0).sum())
        fixed = max(1, used // 4)
        shifted = fixed + (places - fixed + offset_by * (used - fixed)) % max(1, amount - fixed)
        return jnp.zeros((amount,), jnp.int32).at[ranking[jnp.where(places < fixed, places, shifted)]].set(jnp.asarray(sizes, jnp.int32))

    sizes = jnp.where(number % 4 == 0, named(packed, number // 4), named(usual, number - number // 4 - 1))
    mixed = jax.random.permutation(jax.random.fold_in(own, 3), amount)
    source_of, taker = mixed[0:amount // 2 * 2:2], mixed[1:amount // 2 * 2:2]
    margin = jnp.minimum(sizes[source_of] - 1, limit - sizes[taker]) // 2
    margin = jnp.where((source_of == ranking[0]) | (taker == ranking[0]) | (sizes[taker] == 0), 0, jnp.maximum(margin, 0))
    shifted = jax.random.randint(jax.random.fold_in(own, 4), (amount // 2,), 0, 1 << 20) % (margin + 1)
    sizes = sizes.at[source_of].add(-shifted).at[taker].add(shifted)
    members = jnp.searchsorted(jnp.cumsum(sizes), jnp.arange(rows * top), side="right").astype(jnp.int32)
    grid = members.reshape(top, rows).T
    grid = grid[jax.random.permutation(jax.random.fold_in(own, 1), rows)]
    offset_by = jax.random.randint(jax.random.fold_in(own, 2), (rows, 1), 0, top)
    return jnp.take_along_axis(grid, (jnp.arange(top)[None, :] + offset_by) % top, axis=1)


def load_shares(count, total, reach, slope, full):
    portions = [(1 << 20) // math.isqrt(grade ** slope) + 1 for grade in range(1, count + 1)]
    largest = reach if full else min(reach, max(-(-total // count), total * portions[0] // sum(portions)))
    least = 1 if total - largest >= count - 1 else 0
    given, surplus = [largest] + [least] * (count - 1), total - largest - least * (count - 1)
    while surplus > 0:
        movable = [i for i in range(1, count) if given[i] < largest] or [i for i in range(1, count) if given[i] < reach]
        whole, budget = sum([portions[i] for i in movable]), surplus
        for i in movable:
            more = min(reach - given[i], max(1, budget * portions[i] // whole), surplus)
            given[i] = given[i] + more
            surplus = surplus - more
    return np.array(given)


def bell_draw(own_key, extent, deviation, bound, pieces=(), kind=jnp.bfloat16):
    result = deviation * jax.random.normal(own_key, extent, jnp.float32)
    if pieces:
        result = result * levels(own_key, extent, pieces, -0.22, 0.18)
    return jnp.clip(result, -bound, bound).astype(kind)


def setup_inputs(seed: int = 0) -> dict:
    key_of = jax.random.split(jax.random.key(seed), 5)
    samples = bell_draw(key_of[0], (N_IN, SPEC, TAPS), 1.0, 6.0, ((0, 128), (1, 2)))
    destination_keys = jax.random.split(jax.random.fold_in(key_of[1], 1), ROWS_ALL // R_DEV)
    destination_turns = jax.random.permutation(jax.random.fold_in(key_of[1], 3), ROWS_ALL // R_DEV)
    destination = jax.vmap(lambda own, number: deal_out(jax.random.fold_in(key_of[1], 2), own, number, R_DEV, N_GI * N_GJ, 1, CAP, 2))(destination_keys, destination_turns).reshape((ROWS_ALL, 1))
    offset = plant(jax.random.randint(key_of[2], (ROWS_ALL,), 0, TU), jax.random.fold_in(key_of[2], 1), 0, TU - 1).astype(jnp.int32)
    weight = jnp.clip(jnp.exp(math.log(4.0) - 2.7725887 * jax.random.uniform(key_of[3], (ROWS_ALL,), jnp.float32) ** levels(key_of[3], (ROWS_ALL,), ((0, 256),), -0.2, 0.2)), 0.25, 4.0).astype(jnp.bfloat16)
    return dict(samples=samples, destination=destination, offset=offset, weight=weight)


def dft_tables():
    sample_index = jnp.arange(TAPS, dtype=jnp.int32)
    channel_index = jnp.arange(NCHAN, dtype=jnp.int32)
    phase = (channel_index[:, None] * sample_index[None, :] % TAPS).astype(jnp.float32) * (2.0 * math.pi / TAPS)
    return (jnp.cos(phase), -jnp.sin(phase))

def arrange_block(block, halves):
    grouped = block.reshape(N_GI, ROWG, N_GI, N_GJ, IN_DEV).transpose(0, 3, 1, 2, 4)
    return grouped.reshape(N_GI, N_GJ, ROWG, halves, TV)

def reference(samples, destination, offset, weight):
    cosine_table, sine_table = dft_tables()
    widened = samples.astype(jnp.float32)
    real_part = jnp.einsum('nst,ct->cns', widened, cosine_table, precision=lax.Precision.HIGHEST).astype(jnp.bfloat16)
    imag_part = jnp.einsum('nst,ct->cns', widened, sine_table, precision=lax.Precision.HIGHEST).astype(jnp.bfloat16)
    normalize = 1.0 / (NCHAN * math.sqrt(SPEC))
    halves = COLG // TV
    route_table = destination.reshape(N_GI, N_GJ, N_CH, CHAN_DEV, ROWG, halves)
    offset_table = offset.reshape(N_GI, N_GJ, N_CH, CHAN_DEV, ROWG, halves)
    weight_table = weight.astype(jnp.float32).reshape(N_GI, N_GJ, N_CH, CHAN_DEV, ROWG, halves)

    def accumulate(grid_sum, channel):
        band = channel // CHAN_DEV
        local_channel = channel % CHAN_DEV
        real_in = real_part[channel]
        imag_in = imag_part[channel]
        real_vis = (jnp.dot(real_in, real_in.T, preferred_element_type=jnp.float32) + jnp.dot(imag_in, imag_in.T, preferred_element_type=jnp.float32)) * normalize
        imag_vis = (jnp.dot(imag_in, real_in.T, preferred_element_type=jnp.float32) - jnp.dot(real_in, imag_in.T, preferred_element_type=jnp.float32)) * normalize
        rounded = jnp.concatenate([arrange_block(real_vis, halves), arrange_block(imag_vis, halves)], axis=-1).astype(jnp.bfloat16)
        row_values = lax.optimization_barrier(rounded).astype(jnp.float32)
        targets = route_table[:, :, band, local_channel]
        grid_rows = offset_table[:, :, band, local_channel]
        row_weights = weight_table[:, :, band, local_channel]
        grid_sum = grid_sum.at[band, targets, grid_rows].add(row_weights[..., None] * row_values)
        return (grid_sum, None)
    initial = jnp.zeros((N_CH, N_GI * N_GJ, TU, 2 * TV), jnp.float32)
    grid_sum, unused = lax.scan(accumulate, initial, jnp.arange(NCHAN, dtype=jnp.int32))
    return grid_sum
```

```python
import math

import jax
import jax.numpy as jnp
from jax import lax
from jax.experimental import pallas as pl
from jax.experimental.pallas import tpu as pltpu
from jax.sharding import PartitionSpec as P

NCHAN = 16
TAPS = 32
SPEC = 512
GI, GJ, CH = 16, 8, 2
N_IN = 4096
TU = 512
TV = 256
LANES = 128
STEPS = 8
CHUNK = 256
UNROLL = 16
ROWS_CH = 65536
BIG = 1 << 28
WINDOW = 8192
SPARE = GJ * TU * 4


def dft_tables():
    sample_index = jnp.arange(TAPS, dtype=jnp.int32)
    channel_index = jnp.arange(NCHAN, dtype=jnp.int32)
    phase = (channel_index[:, None] * sample_index[None, :] % TAPS).astype(jnp.float32) * (
        2.0 * math.pi / TAPS
    )
    return (jnp.cos(phase), -jnp.sin(phase))


def grid_kernel(starts, place, rows, cells, weights, *refs):
    re_all, im_all, (keep, send), scratch = refs[:5], refs[5:10], refs[10:12], refs[12:]
    volts, row_at, cell_at, weight_at, wide, picked, vis, acc, sems, list_sems = scratch
    normalize = 1.0 / (NCHAN * math.sqrt(SPEC))
    copies = []

    def fetch(source, row, count, lane):
        target = volts.at[pl.ds(row, count), pl.ds(lane, SPEC)]
        copy = pltpu.make_async_copy(source, target, sems.at[len(copies)])
        copies.append((copy, row, count, lane))
        copy.start()

    for s, ref in zip((0, 1, 2, 3, 3.5), re_all):
        fetch(ref, int(s * 1024), ref.shape[0], 0)
    for s, ref in zip((0, 1, 2, 3, 3), im_all):
        first = 2 if ref is im_all[4] else 0
        for part in range(ref.shape[0] // 256):
            fetch(ref.at[pl.ds(part * 256, 256)], (first + part) * 1024 + s * 256, 256, SPEC)

    def lists(turn):
        window = pl.ds(pl.multiple_of(turn * WINDOW, WINDOW), WINDOW)
        return [
            pltpu.make_async_copy(source.at[window], target.at[pl.ds(0, WINDOW)], list_sems.at[i])
            for i, (source, target) in enumerate(((rows, row_at), (cells, cell_at), (weights, weight_at)))
        ]

    for i in range(UNROLL):
        row_at[WINDOW + i] = 0
        cell_at[WINDOW + i] = 0
        weight_at[WINDOW + i] = 0.0

    @pl.loop(0, GJ * TU * 4 // 512)
    def _(r):
        acc[pl.ds(pl.multiple_of(r * 512, 512), 512), :] = jnp.zeros((512, LANES), jnp.float32)

    for copy, row, count, lane in copies:
        copy.wait()

        @pl.loop(0, count // 64)
        def _(r, row=row, lane=lane):
            block = volts[pl.ds(pl.multiple_of(row + r * 64, 64), 64), pl.ds(lane, SPEC)].astype(jnp.float32)
            for k in range(4):
                wide[pl.ds((row + r * 64) * STEPS + lane // LANES + k, 64, stride=STEPS), :] = block[
                    :, k * LANES:(k + 1) * LANES
                ]

    def dot(a, b):
        return lax.dot_general(a, b, (((1,), (1,)), ((), ())), preferred_element_type=jnp.float32)

    @pl.loop(0, (starts[2 * GJ] + WINDOW - 1) // WINDOW)
    def _(turn):
        for copy in lists(turn):
            copy.start()
        for copy in lists(turn):
            copy.wait()

        @pl.loop(0, 2 * GJ)
        def _(group):
            column, half = group // 2, group % 2
            blocks = [
                volts[pl.ds(pl.multiple_of(place[2 + half * 8 + p] * 256 + column * 32, 32), 32), :]
                for p in range(8)
            ]
            columns = jnp.concatenate(blocks, axis=0)
            c_re, c_im = columns[:, :512], columns[:, 512:]
            first = jnp.maximum(starts[group] - turn * WINDOW, 0)
            last = jnp.minimum(starts[group + 1] - turn * WINDOW, WINDOW)

            @pl.loop(0, (jnp.maximum(last - first, 0) + CHUNK - 1) // CHUNK)
            def _(step):
                base = first + step * CHUNK
                count = jnp.minimum(last - base, CHUNK)
                rounds = (count + UNROLL - 1) // UNROLL

                @pl.loop(0, rounds)
                def _(r):
                    at = r * UNROLL
                    for i in range(UNROLL):
                        row = pl.multiple_of(row_at[base + at + i], STEPS)
                        picked[pl.ds(pl.multiple_of((at + i) * STEPS, STEPS), STEPS), :] = wide[pl.ds(row, STEPS), :]

                pieces = [picked[pl.ds(k, CHUNK, stride=STEPS), :].astype(jnp.bfloat16) for k in range(STEPS)]
                r_re = jnp.concatenate(pieces[:4], axis=1)
                r_im = jnp.concatenate(pieces[4:], axis=1)
                real = (dot(r_re, c_re) + dot(r_im, c_im)) * normalize
                imag = (dot(r_im, c_re) - dot(r_re, c_im)) * normalize
                for j, part in enumerate((real[:, :LANES], real[:, LANES:], imag[:, :LANES], imag[:, LANES:])):
                    vis[pl.ds(j, CHUNK, stride=4), :] = part.astype(jnp.bfloat16).astype(jnp.float32)

                @pl.loop(0, rounds)
                def _(r):
                    at = r * UNROLL
                    where, load, old, new = [], [], [], []
                    for i in range(UNROLL):
                        used = at + i < count
                        cell = jnp.where(used, cell_at[base + at + i], SPARE)
                        where.append(pl.multiple_of(cell, 4))
                        load.append(jnp.where(used, weight_at[base + at + i], 0.0))
                        old.append(acc[pl.ds(where[i], 4), :])
                        new.append(load[i] * vis[pl.ds(pl.multiple_of((at + i) * 4, 4), 4), :])
                    total = old[0] + new[0]
                    sums = [total]
                    for i in range(1, UNROLL):
                        total = jnp.where(where[i] == where[i - 1], total, old[i]) + new[i]
                        sums.append(total)
                    for i in range(UNROLL):
                        acc[pl.ds(where[i], 4), :] = sums[i]

    z, core = place[0], place[1]
    for k in range(4):
        tile = 2 * lax.rem(z + k, 4)
        for j in range(4):
            lanes = slice(j * LANES, (j + 1) * LANES)
            keep[k, :, lanes] = acc[pl.ds((tile + core) * (TU * 4) + j, TU, stride=4), :]
            send[k, :, lanes] = acc[pl.ds((tile + 1 - core) * (TU * 4) + j, TU, stride=4), :].astype(jnp.bfloat16)


def grid_rows(starts, place, rows, cells, weights, *volts):
    smem = pl.BlockSpec(memory_space=pltpu.SMEM)
    vmem = pl.BlockSpec(memory_space=pltpu.VMEM)
    return pl.pallas_call(
        grid_kernel,
        out_shape=(
            jax.ShapeDtypeStruct((4, TU, 2 * TV), jnp.float32),
            jax.ShapeDtypeStruct((4, TU, 2 * TV), jnp.bfloat16),
        ),
        in_specs=[smem, smem] + [pl.BlockSpec(memory_space=pl.ANY)] * 13,
        out_specs=(vmem, vmem),
        scratch_shapes=[
            pltpu.VMEM((N_IN, 2 * SPEC), jnp.bfloat16),
            pltpu.SMEM((WINDOW + UNROLL,), jnp.int32),
            pltpu.SMEM((WINDOW + UNROLL,), jnp.int32),
            pltpu.SMEM((WINDOW + UNROLL,), jnp.float32),
            pltpu.VMEM((N_IN * STEPS, LANES), jnp.float32),
            pltpu.VMEM((CHUNK * STEPS, LANES), jnp.float32),
            pltpu.VMEM((CHUNK * 4, LANES), jnp.float32),
            pltpu.VMEM((SPARE + 8, LANES), jnp.float32),
            pltpu.SemaphoreType.DMA((21,)),
            pltpu.SemaphoreType.DMA((3,)),
        ],
        compiler_params=pltpu.CompilerParams(vmem_limit_bytes=56 * 1024 * 1024),
        name="grid_rows",
    )(starts, place, rows, cells, weights, *volts)


def along(axis, step):
    pairs = []
    for y in range(4):
        for x in range(4):
            to = (y + step) % 4 * 4 + x if axis == "y" else y * 4 + (x + step) % 4
            pairs.append((y * 4 + x, to))
    return pairs


def spread_ring(block, axis):
    rows = block.shape[0] // 2
    before = lax.ppermute(block, "gi", along(axis, 1))
    after = lax.ppermute(block, "gi", along(axis, -1))
    across_low = lax.ppermute(before[:rows], "gi", along(axis, 1))
    across_high = lax.ppermute(after[rows:], "gi", along(axis, -1))
    return block, before, after, across_low, across_high


def spread_direct(block, axis):
    return jnp.stack([block] + [lax.ppermute(block, "gi", along(axis, step)) for step in (1, -1, 2)])


def shards(samples, destination, offset, weight):
    gi, gj, ch = lax.axis_index("gi"), lax.axis_index("gj"), lax.axis_index("ch")
    cosine_table, sine_table = dft_tables()
    widened = samples.astype(jnp.float32)
    tables = jnp.stack([cosine_table, sine_table]).reshape(2, CH, GJ, TAPS)
    spectra = jnp.einsum("nst,kblt->lbkns", widened, tables, precision=lax.Precision.HIGHEST)
    spectra = spectra.astype(jnp.bfloat16).reshape(GJ, CH, 64, 256)
    route = jnp.stack([destination[:, 0], offset >> 8, offset & 255]).astype(jnp.bfloat16)
    route = jnp.concatenate([route, weight[None]]).reshape(4, GJ, 2, 256).transpose(1, 0, 2, 3)
    route = jnp.broadcast_to(route.reshape(GJ, 1, 8, 256), (GJ, CH, 8, 256))
    outgoing = jnp.concatenate([spectra, route], axis=2).reshape(GJ * CH, 72, 256)
    turned = lax.all_to_all(outgoing, ("gj", "ch"), split_axis=0, concat_axis=0, tiled=True)
    turned = turned.reshape(GJ, CH, 72, 256)
    route = lax.dynamic_index_in_dim(turned[:, :, 64:], ch, 1, keepdims=False)
    route = route.reshape(GJ, 4, 2, 256).transpose(1, 0, 2, 3).reshape(4, 16, 256)
    volts = turned[:, :, :64].reshape(GJ, CH, 2, 32, 256).transpose(2, 0, 3, 1, 4).reshape(2, 256, SPEC)

    route = spread_direct(spread_direct(route, "x"), "y")
    y, x = gi // 4, gi % 4

    def slot(step):
        step = step & 3
        return jnp.where(step == 0, 0, jnp.where(step == 3, 1, jnp.where(step == 1, 2, 3)))

    slot_of = slot(jnp.arange(16, dtype=jnp.int32) // 4 - y) * 4 + slot(jnp.arange(16, dtype=jnp.int32) % 4 - x)

    def join(parts):
        return jnp.concatenate(parts)

    re_x = join(spread_ring(volts[0], "x"))
    im_y = join(spread_ring(volts[1], "y"))
    re_all = spread_ring(re_x, "y")
    im_all = spread_ring(im_y, "x")

    route = route.reshape(16, 4, 4096).astype(jnp.float32)
    loads = route[:, 3].reshape(ROWS_CH)
    tile = route[:, 0].astype(jnp.int32).reshape(ROWS_CH)
    shift = (route[:, 1] * 256.0 + route[:, 2]).astype(jnp.int32).reshape(ROWS_CH)
    index = jnp.arange(ROWS_CH, dtype=jnp.int32)
    column = (index // 512 % 8) * 2 + index % 2
    row = index // 4096 * 256 + index // 2 % 256
    keys = column * (1 << 24) + ((tile % GJ) * TU + shift) * (1 << 12) + row
    keys = jnp.where(tile // GJ == gi, keys, BIG)
    starts = jnp.sum(
        (keys[None, :] < (jnp.arange(17, dtype=jnp.int32) * (1 << 24))[:, None]).astype(jnp.int32), axis=1
    )
    keys, loads = lax.sort((keys, loads), num_keys=1)
    place = jnp.concatenate([jnp.stack([gj // 2, gj % 2]).astype(jnp.int32), slot_of])
    rows, cells = (keys & (N_IN - 1)) * STEPS, ((keys >> 12) & (N_IN - 1)) * 4
    keep, send = grid_rows(starts, place, rows, cells, loads, *re_all, *im_all)

    got = lax.ppermute(send, "gj", [(j, j ^ 1) for j in range(GJ)])
    pair = keep + got.astype(jnp.float32)

    def step(block, by):
        turn = [(z * 2 + c, (z + by) % 4 * 2 + c) for z in range(4) for c in range(2)]
        return lax.ppermute(block.astype(jnp.bfloat16), "gj", turn).astype(jnp.float32)

    half = TU // 2
    low, high = step(pair[2, :half], 1), step(pair[2, half:], -1)
    ahead = step(jnp.concatenate([pair[1, :half] + low, pair[1, half:]]), 1)
    behind = step(jnp.concatenate([pair[3, :half], pair[3, half:] + high]), -1)
    out = pair[0] + (ahead + behind)
    return out[None, None]


def solution(mesh):
    in_specs = (
        P(("gi", "gj"), "ch", None),
        P(("gi", "gj", "ch"), None),
        P(("gi", "gj", "ch")),
        P(("gi", "gj", "ch")),
    )
    out_specs = P("ch", ("gi", "gj"), None, None)
    return jax.shard_map(shards, mesh=mesh, in_specs=in_specs, out_specs=out_specs, check_vma=False)
```

```python
import functools
import math

import jax
import jax.numpy as jnp
from jax import lax
from jax.experimental import pallas as pl
from jax.experimental.pallas import tpu as pltpu
from jax.sharding import PartitionSpec as P

NCHAN = 16
TAPS = 32
SPEC = 512
GI, GJ, CH = 16, 8, 2
N_IN = 4096
TU = 512
TV = 256
LANES = 128
STEPS = 8
CHUNKS = (384,)
UNROLL = 16
ROWS_CH = 65536
BIG = 1 << 29
WINDOW = 8192
PARTS = ((2, 1, 3, 0),)


def dft_tables():
    sample_index = jnp.arange(TAPS, dtype=jnp.int32)
    channel_index = jnp.arange(NCHAN, dtype=jnp.int32)
    phase = (channel_index[:, None] * sample_index[None, :] % TAPS).astype(jnp.float32) * (
        2.0 * math.pi / TAPS
    )
    return (jnp.cos(phase), -jnp.sin(phase))


def grid_kernel(part, starts, place, rows, cells, weights, *refs):
    re_all, im_all, (keep, send), scratch = refs[:5], refs[5:10], refs[10:12], refs[12:]
    volts, row_at, cell_at, weight_at, wide, picked, vis, acc, sems, list_sems = scratch
    normalize = 1.0 / (NCHAN * math.sqrt(SPEC))
    copies = []
    tiles = 2 * len(PARTS[part])
    chunk = CHUNKS[part]
    spare = tiles * TU * 4
    groups = 2 * GJ * part

    def fetch(source, row, count, lane):
        target = volts.at[pl.ds(row, count), pl.ds(lane, SPEC)]
        copy = pltpu.make_async_copy(source, target, sems.at[len(copies)])
        copies.append((copy, row, count, lane))
        copy.start()

    for s, ref in zip((0, 1, 2, 3, 3.5), re_all):
        fetch(ref, int(s * 1024), ref.shape[0], 0)
    for s, ref in zip((0, 1, 2, 3, 3), im_all):
        first = 2 if ref is im_all[4] else 0
        for part in range(ref.shape[0] // 256):
            fetch(ref.at[pl.ds(part * 256, 256)], (first + part) * 1024 + s * 256, 256, SPEC)

    def lists(turn):
        window = pl.ds(pl.multiple_of(turn * WINDOW, WINDOW), WINDOW)
        return [
            pltpu.make_async_copy(source.at[window], target.at[pl.ds(0, WINDOW)], list_sems.at[i])
            for i, (source, target) in enumerate(((rows, row_at), (cells, cell_at), (weights, weight_at)))
        ]

    for i in range(UNROLL):
        row_at[WINDOW + i] = 0
        cell_at[WINDOW + i] = 0
        weight_at[WINDOW + i] = 0.0

    @pl.loop(0, spare // 512)
    def _(r):
        acc[pl.ds(pl.multiple_of(r * 512, 512), 512), :] = jnp.zeros((512, LANES), jnp.float32)

    for copy, row, count, lane in copies:
        copy.wait()

        @pl.loop(0, count // 64)
        def _(r, row=row, lane=lane):
            block = volts[pl.ds(pl.multiple_of(row + r * 64, 64), 64), pl.ds(lane, SPEC)].astype(jnp.float32)
            for k in range(4):
                wide[pl.ds((row + r * 64) * STEPS + lane // LANES + k, 64, stride=STEPS), :] = block[
                    :, k * LANES:(k + 1) * LANES
                ]

    def dot(a, b):
        return lax.dot_general(a, b, (((1,), (1,)), ((), ())), preferred_element_type=jnp.float32)

    @pl.loop(starts[groups] // WINDOW, (starts[groups + 2 * GJ] + WINDOW - 1) // WINDOW)
    def _(turn):
        for copy in lists(turn):
            copy.start()
        for copy in lists(turn):
            copy.wait()

        @pl.loop(0, 2 * GJ)
        def _(group):
            column, half = group // 2, group % 2
            blocks = [
                volts[pl.ds(pl.multiple_of(place[half * 8 + p] * 256 + column * 32, 32), 32), :]
                for p in range(8)
            ]
            columns = jnp.concatenate(blocks, axis=0)
            first = jnp.maximum(starts[groups + group] - turn * WINDOW, 0)
            last = jnp.minimum(starts[groups + group + 1] - turn * WINDOW, WINDOW)

            @pl.loop(0, (jnp.maximum(last - first, 0) + chunk - 1) // chunk)
            def _(step):
                base = first + step * chunk
                count = jnp.minimum(last - base, chunk)
                rounds = (count + UNROLL - 1) // UNROLL

                @pl.loop(0, rounds)
                def _(r):
                    at = r * UNROLL
                    for i in range(UNROLL):
                        row = pl.multiple_of(row_at[base + at + i], STEPS)
                        picked[pl.ds(pl.multiple_of((at + i) * STEPS, STEPS), STEPS), :] = wide[pl.ds(row, STEPS), :]

                pieces = [picked[pl.ds(k, chunk, stride=STEPS), :].astype(jnp.bfloat16) for k in range(STEPS)]
                turned = pieces[4:] + [-piece for piece in pieces[:4]]
                both = jnp.concatenate([jnp.concatenate(pieces, axis=1), jnp.concatenate(turned, axis=1)], axis=0)
                both = dot(both, columns) * normalize
                real, imag = both[:chunk], both[chunk:]
                for j, part in enumerate((real[:, :LANES], real[:, LANES:], imag[:, :LANES], imag[:, LANES:])):
                    vis[pl.ds(j, chunk, stride=4), :] = part.astype(jnp.bfloat16).astype(jnp.float32)

                def add(at, used):
                    where, load, old, new = [], [], [], []
                    for i in range(UNROLL):
                        cell, weight = cell_at[base + at + i], weight_at[base + at + i]
                        if used is not None:
                            cell = jnp.where(i < used, cell, spare)
                            weight = jnp.where(i < used, weight, 0.0)
                        where.append(pl.multiple_of(cell, 4))
                        old.append(acc[pl.ds(where[i], 4), :])
                        new.append(weight * vis[pl.ds(pl.multiple_of((at + i) * 4, 4), 4), :])
                    sums = [old[0] + new[0]]
                    for i in range(1, UNROLL):
                        sums.append(jnp.where(where[i] == where[i - 1], sums[-1], old[i]) + new[i])
                    for i in range(UNROLL):
                        acc[pl.ds(where[i], 4), :] = sums[i]

                full = count // UNROLL

                @pl.loop(0, full)
                def _(r):
                    add(r * UNROLL, None)

                @pl.when(count > full * UNROLL)
                def _():
                    add(full * UNROLL, count - full * UNROLL)

    for k in range(tiles // 2):
        for j in range(4):
            lanes = slice(j * LANES, (j + 1) * LANES)
            keep[k, :, lanes] = acc[pl.ds(2 * k * TU * 4 + j, TU, stride=4), :]
            send[k, :, lanes] = acc[pl.ds((2 * k + 1) * TU * 4 + j, TU, stride=4), :].astype(jnp.bfloat16)


def grid_rows(part, starts, place, rows, cells, weights, *volts):
    smem = pl.BlockSpec(memory_space=pltpu.SMEM)
    vmem = pl.BlockSpec(memory_space=pltpu.VMEM)
    count = len(PARTS[part])
    return pl.pallas_call(
        functools.partial(grid_kernel, part),
        out_shape=(
            jax.ShapeDtypeStruct((count, TU, 2 * TV), jnp.float32),
            jax.ShapeDtypeStruct((count, TU, 2 * TV), jnp.bfloat16),
        ),
        in_specs=[smem, smem] + [pl.BlockSpec(memory_space=pl.ANY)] * 13,
        out_specs=(vmem, vmem),
        scratch_shapes=[
            pltpu.VMEM((N_IN, 2 * SPEC), jnp.bfloat16),
            pltpu.SMEM((WINDOW + UNROLL,), jnp.int32),
            pltpu.SMEM((WINDOW + UNROLL,), jnp.int32),
            pltpu.SMEM((WINDOW + UNROLL,), jnp.float32),
            pltpu.VMEM((N_IN * STEPS, LANES), jnp.float32),
            pltpu.VMEM((CHUNKS[part] * STEPS, LANES), jnp.float32),
            pltpu.VMEM((CHUNKS[part] * 4, LANES), jnp.float32),
            pltpu.VMEM((2 * count * TU * 4 + 8, LANES), jnp.float32),
            pltpu.SemaphoreType.DMA((21,)),
            pltpu.SemaphoreType.DMA((3,)),
        ],
        compiler_params=pltpu.CompilerParams(vmem_limit_bytes=56 * 1024 * 1024),
        cost_estimate=pl.CostEstimate(flops=count << 30, bytes_accessed=64 << 20, transcendentals=0),
        name="grid_rows",
    )(starts, place, rows, cells, weights, *volts)


def along(axis, step):
    pairs = []
    for y in range(4):
        for x in range(4):
            to = (y + step) % 4 * 4 + x if axis == "y" else y * 4 + (x + step) % 4
            pairs.append((y * 4 + x, to))
    return pairs


def spread_near(block, axis):
    return block, lax.ppermute(block, "gi", along(axis, 1)), lax.ppermute(block, "gi", along(axis, -1))


def spread_far(near, axis):
    block, before, after = near
    half = block.shape[0] // 2
    low = lax.ppermute(before[:half], "gi", along(axis, 1))
    high = lax.ppermute(after[half:], "gi", along(axis, -1))
    return [block, before, after, low, high]


def spread_direct(block, axis):
    return jnp.stack([block] + [lax.ppermute(block, "gi", along(axis, step)) for step in (1, -1, 2)])


def shards(samples, destination, offset, weight):
    gi, gj, ch = lax.axis_index("gi"), lax.axis_index("gj"), lax.axis_index("ch")
    cosine_table, sine_table = dft_tables()
    widened = samples.astype(jnp.float32)
    tables = jnp.stack([cosine_table, sine_table]).reshape(2, CH, GJ, TAPS)
    spectra = jnp.einsum("nst,kblt->lbkns", widened, tables, precision=lax.Precision.HIGHEST)
    spectra = spectra.astype(jnp.bfloat16).reshape(GJ, CH, 64, 256)
    route = jnp.stack([destination[:, 0], offset >> 8, offset & 255]).astype(jnp.bfloat16)
    route = jnp.concatenate([route, weight[None]]).reshape(4, GJ, 2, 256).transpose(1, 0, 2, 3)
    route = jnp.broadcast_to(route.reshape(GJ, 1, 8, 256), (GJ, CH, 8, 256))
    outgoing = jnp.concatenate([spectra, route], axis=2).reshape(GJ * CH, 72, 256)
    turned = lax.all_to_all(outgoing, ("gj", "ch"), split_axis=0, concat_axis=0, tiled=True)
    turned = turned.reshape(GJ, CH, 72, 256)
    route = lax.dynamic_index_in_dim(turned[:, :, 64:], ch, 1, keepdims=False)
    route = route.reshape(GJ, 4, 2, 256).transpose(1, 0, 2, 3).reshape(4, 16, 256)
    volts = turned[:, :, :64].reshape(GJ, CH, 2, 32, 256).transpose(2, 0, 3, 1, 4).reshape(2, 256, SPEC)

    route = spread_direct(spread_direct(route, "x"), "y")
    y, x = gi // 4, gi % 4

    def slot(step):
        step = step & 3
        return jnp.where(step == 0, 0, jnp.where(step == 3, 1, jnp.where(step == 1, 2, 3)))

    slot_of = slot(jnp.arange(16, dtype=jnp.int32) // 4 - y) * 4 + slot(jnp.arange(16, dtype=jnp.int32) % 4 - x)

    re_x = spread_direct(volts[0], "x").reshape(1024, SPEC)
    im_y = spread_direct(volts[1], "y").reshape(1024, SPEC)

    route = route.reshape(16, 4, 4096).astype(jnp.float32)
    loads = route[:, 3].reshape(ROWS_CH)
    tile = route[:, 0].astype(jnp.int32).reshape(ROWS_CH)
    shift = (route[:, 1] * 256.0 + route[:, 2]).astype(jnp.int32).reshape(ROWS_CH)
    index = jnp.arange(ROWS_CH, dtype=jnp.int32)
    column = (index // 512 % 8) * 2 + index % 2
    row = index // 4096 * 256 + index // 2 % 256
    ahead = ((tile % GJ) // 2 - gj // 2) & 3
    other = (tile % 2) ^ (gj % 2)
    where = jnp.where(ahead == 0, 3, jnp.where(ahead == 3, 2, jnp.where(ahead == 1, 1, 0))) * 2 + other
    keys = column * (1 << 24) + (where * TU + shift) * (1 << 12) + row
    keys = jnp.where(tile // GJ == gi, keys, BIG)
    edges = jnp.arange(2 * GJ * len(PARTS) + 1, dtype=jnp.int32) * (1 << 24)
    starts = jnp.sum((keys[None, :] < edges[:, None]).astype(jnp.int32), axis=1)
    keys, loads, re_x, im_y = lax.optimization_barrier((keys, loads, re_x, im_y))
    re_near = spread_near(re_x, "y")
    im_near = spread_near(im_y, "x")
    keys, loads = lax.sort((keys, loads), num_keys=1, is_stable=False)
    rows, cells = (keys & (N_IN - 1)) * STEPS, ((keys >> 12) & (N_IN - 1)) * 4
    rows, cells, loads, re_near, im_near = lax.optimization_barrier((rows, cells, loads, re_near, im_near))
    volts = spread_far(re_near, "y") + spread_far(im_near, "x")

    keep, send = grid_rows(0, starts, slot_of, rows, cells, loads, *volts)
    got = lax.ppermute(send, "gj", [(j, j ^ 1) for j in range(GJ)])
    pair = keep + got.astype(jnp.float32)

    def step(block, by):
        turn = [(z * 2 + c, (z + by) % 4 * 2 + c) for z in range(4) for c in range(2)]
        return lax.ppermute(block.astype(jnp.bfloat16), "gj", turn)

    half = TU // 2
    low, high = step(pair[0, :half], 1), step(pair[0, half:], -1)
    ahead = step(jnp.concatenate([pair[1, :half] + low.astype(jnp.float32), pair[1, half:]]), 1)
    behind = step(jnp.concatenate([pair[2, :half], pair[2, half:] + high.astype(jnp.float32)]), -1)

    out = pair[3] + (ahead.astype(jnp.float32) + behind.astype(jnp.float32))
    return out[None, None]


def solution(mesh):
    in_specs = (
        P(("gi", "gj"), "ch", None),
        P(("gi", "gj", "ch"), None),
        P(("gi", "gj", "ch")),
        P(("gi", "gj", "ch")),
    )
    out_specs = P("ch", ("gi", "gj"), None, None)
    return jax.shard_map(shards, mesh=mesh, in_specs=in_specs, out_specs=out_specs, check_vma=False)
```

```python
import math

import jax
import jax.numpy as jnp
from jax import lax
from jax.experimental import pallas as pl
from jax.experimental.pallas import tpu as pltpu
from jax.sharding import PartitionSpec as P

NCHAN = 16
TAPS = 32
SPEC = 512
GI, GJ, CH = 16, 8, 2
N_IN = 4096
TU = 512
TV = 256
LANES = 128
STEPS = 8
CHUNK = 384
UNROLL = 16
ROWS_CH = 65536
BIG = 1 << 29
WINDOW = 8192
SPARE = GJ * TU * 4


def dft_tables():
    sample_index = jnp.arange(TAPS, dtype=jnp.int32)
    channel_index = jnp.arange(NCHAN, dtype=jnp.int32)
    phase = (channel_index[:, None] * sample_index[None, :] % TAPS).astype(jnp.float32) * (
        2.0 * math.pi / TAPS
    )
    return (jnp.cos(phase), -jnp.sin(phase))


def grid_kernel(starts, place, rows, cells, weights, *refs):
    re_all, im_all, outs, scratch = refs[:5], refs[5:10], refs[10:14], refs[14:]
    volts, row_at, cell_at, weight_at, wide, picked, vis, acc, sems, list_sems = scratch
    normalize = 1.0 / (NCHAN * math.sqrt(SPEC))
    copies = []

    def fetch(source, row, count, lane):
        target = volts.at[pl.ds(row, count), pl.ds(lane, SPEC)]
        copy = pltpu.make_async_copy(source, target, sems.at[len(copies)])
        copies.append((copy, row, count, lane))
        copy.start()

    for at, ref in zip((0, 1, 2, 3, 3.5), re_all):
        fetch(ref, int(at * 1024), ref.shape[0], 0)
    for at, ref in zip((0, 1, 2, 3, 3), im_all):
        first = 2 if ref is im_all[4] else 0
        for part in range(ref.shape[0] // 256):
            fetch(ref.at[pl.ds(part * 256, 256)], (first + part) * 1024 + at * 256, 256, SPEC)

    def lists(turn):
        window = pl.ds(pl.multiple_of(turn * WINDOW, WINDOW), WINDOW)
        return [
            pltpu.make_async_copy(source.at[window], target.at[pl.ds(0, WINDOW)], list_sems.at[i])
            for i, (source, target) in enumerate(((rows, row_at), (cells, cell_at), (weights, weight_at)))
        ]

    for copy in lists(0):
        copy.start()

    for i in range(UNROLL):
        row_at[WINDOW + i] = 0
        cell_at[WINDOW + i] = 0
        weight_at[WINDOW + i] = 0.0

    @pl.loop(0, SPARE // 512)
    def _(r):
        acc[pl.ds(pl.multiple_of(r * 512, 512), 512), :] = jnp.zeros((512, LANES), jnp.float32)

    for copy, row, count, lane in copies:
        copy.wait()

        @pl.loop(0, count // 64)
        def _(r, row=row, lane=lane):
            block = volts[pl.ds(pl.multiple_of(row + r * 64, 64), 64), pl.ds(lane, SPEC)].astype(jnp.float32)
            for k in range(4):
                wide[pl.ds((row + r * 64) * STEPS + lane // LANES + k, 64, stride=STEPS), :] = block[
                    :, k * LANES:(k + 1) * LANES
                ]

    def dot(a, b):
        return lax.dot_general(a, b, (((1,), (1,)), ((), ())), preferred_element_type=jnp.float32)

    @pl.loop(0, jnp.maximum((starts[2 * GJ] + WINDOW - 1) // WINDOW, 1))
    def _(turn):
        @pl.when(turn > 0)
        def _():
            for copy in lists(turn):
                copy.start()

        for copy in lists(turn):
            copy.wait()

        @pl.loop(0, 2 * GJ)
        def _(group):
            column, half = group // 2, group % 2
            blocks = [
                volts[pl.ds(pl.multiple_of(place[half * 8 + p] * 256 + column * 32, 32), 32), :]
                for p in range(8)
            ]
            columns = jnp.concatenate(blocks, axis=0)
            first = jnp.maximum(starts[group] - turn * WINDOW, 0)
            last = jnp.minimum(starts[group + 1] - turn * WINDOW, WINDOW)

            @pl.loop(0, (jnp.maximum(last - first, 0) + CHUNK - 1) // CHUNK)
            def _(step):
                base = first + step * CHUNK
                count = jnp.minimum(last - base, CHUNK)
                rounds = (count + UNROLL - 1) // UNROLL

                @pl.loop(0, rounds)
                def _(r):
                    at = r * UNROLL
                    for i in range(UNROLL):
                        row = pl.multiple_of(row_at[base + at + i], STEPS)
                        picked[pl.ds(pl.multiple_of((at + i) * STEPS, STEPS), STEPS), :] = wide[pl.ds(row, STEPS), :]

                pieces = [picked[pl.ds(k, CHUNK, stride=STEPS), :].astype(jnp.bfloat16) for k in range(STEPS)]
                turned = pieces[4:] + [-piece for piece in pieces[:4]]
                both = jnp.concatenate([jnp.concatenate(pieces, axis=1), jnp.concatenate(turned, axis=1)], axis=0)
                both = dot(both, columns) * normalize
                real, imag = both[:CHUNK], both[CHUNK:]
                for j, part in enumerate((real[:, :LANES], real[:, LANES:], imag[:, :LANES], imag[:, LANES:])):
                    vis[pl.ds(j, CHUNK, stride=4), :] = part.astype(jnp.bfloat16).astype(jnp.float32)

                def add(at, used):
                    where, load, old, new = [], [], [], []
                    for i in range(UNROLL):
                        cell, weight = cell_at[base + at + i], weight_at[base + at + i]
                        if used is not None:
                            cell = jnp.where(i < used, cell, SPARE)
                            weight = jnp.where(i < used, weight, 0.0)
                        where.append(pl.multiple_of(cell, 4))
                        old.append(acc[pl.ds(where[i], 4), :])
                        new.append(weight * vis[pl.ds(pl.multiple_of((at + i) * 4, 4), 4), :])
                    sums = [old[0] + new[0]]
                    for i in range(1, UNROLL):
                        sums.append(jnp.where(where[i] == where[i - 1], sums[-1], old[i]) + new[i])
                    for i in range(UNROLL):
                        acc[pl.ds(where[i], 4), :] = sums[i]

                full = count // UNROLL

                @pl.loop(0, full)
                def _(r):
                    add(r * UNROLL, None)

                @pl.when(count > full * UNROLL)
                def _():
                    add(full * UNROLL, count - full * UNROLL)

    for k in range(4):
        keep, send = outs[:2] if k == 0 else outs[2:]
        to = max(k - 1, 0)
        for j in range(4):
            lanes = slice(j * LANES, (j + 1) * LANES)
            keep[to, :, lanes] = acc[pl.ds(2 * k * TU * 4 + j, TU, stride=4), :]
            send[to, :, lanes] = acc[pl.ds((2 * k + 1) * TU * 4 + j, TU, stride=4), :].astype(jnp.bfloat16)


def grid_rows(starts, place, rows, cells, weights, *volts):
    smem = pl.BlockSpec(memory_space=pltpu.SMEM)
    vmem = pl.BlockSpec(memory_space=pltpu.VMEM)
    return pl.pallas_call(
        grid_kernel,
        out_shape=tuple(
            jax.ShapeDtypeStruct((count, TU, 2 * TV), dtype)
            for count in (1, 3)
            for dtype in (jnp.float32, jnp.bfloat16)
        ),
        in_specs=[smem, smem] + [pl.BlockSpec(memory_space=pl.ANY)] * 13,
        out_specs=(vmem,) * 4,
        scratch_shapes=[
            pltpu.VMEM((N_IN, 2 * SPEC), jnp.bfloat16),
            pltpu.SMEM((WINDOW + UNROLL,), jnp.int32),
            pltpu.SMEM((WINDOW + UNROLL,), jnp.int32),
            pltpu.SMEM((WINDOW + UNROLL,), jnp.float32),
            pltpu.VMEM((N_IN * STEPS, LANES), jnp.float32),
            pltpu.VMEM((CHUNK * STEPS, LANES), jnp.float32),
            pltpu.VMEM((CHUNK * 4, LANES), jnp.float32),
            pltpu.VMEM((SPARE + 8, LANES), jnp.float32),
            pltpu.SemaphoreType.DMA((21,)),
            pltpu.SemaphoreType.DMA((3,)),
        ],
        compiler_params=pltpu.CompilerParams(vmem_limit_bytes=56 * 1024 * 1024),
        cost_estimate=pl.CostEstimate(flops=1 << 33, bytes_accessed=64 << 20, transcendentals=0),
        name="grid_rows",
    )(starts, place, rows, cells, weights, *volts)


def along(axis, step):
    pairs = []
    for y in range(4):
        for x in range(4):
            to = (y + step) % 4 * 4 + x if axis == "y" else y * 4 + (x + step) % 4
            pairs.append((y * 4 + x, to))
    return pairs


def spread_direct(block, axis):
    return [block] + [lax.ppermute(block, "gi", along(axis, step)) for step in (1, -1, 2)]


def spread_near(block, axis):
    return block, lax.ppermute(block, "gi", along(axis, 1)), lax.ppermute(block, "gi", along(axis, -1))


def halves_kernel(*refs):
    for source, target in zip(refs[:4], refs[4:]):
        target[...] = source[...]


def halves(*blocks):
    return pl.pallas_call(
        halves_kernel,
        grid=(2,),
        out_shape=(jax.ShapeDtypeStruct((512, SPEC), jnp.bfloat16),) * 4,
        in_specs=[pl.BlockSpec((256, SPEC), lambda i, at=at: (at + i, 0)) for at in (0, 2, 0, 2)],
        out_specs=(pl.BlockSpec((256, SPEC), lambda i: (i, 0)),) * 4,
        name="halves",
    )(*blocks)


def spread_far(re_near, im_near):
    parts = halves(*re_near[1:], *im_near[1:])
    far = [
        lax.ppermute(part, "gi", along(axis, by))
        for part, axis, by in zip(parts, ("y", "y", "x", "x"), (1, -1, 1, -1))
    ]
    return [*re_near, *far[:2], *im_near, *far[2:]]


def shards(samples, destination, offset, weight):
    gi, gj, ch = lax.axis_index("gi"), lax.axis_index("gj"), lax.axis_index("ch")
    cosine_table, sine_table = dft_tables()
    widened = samples.astype(jnp.float32)
    tables = jnp.stack([cosine_table, sine_table]).reshape(2, CH, GJ, TAPS)
    spectra = jnp.einsum("nst,kblt->lbkns", widened, tables, precision=lax.Precision.HIGHEST)
    spectra = spectra.astype(jnp.bfloat16).reshape(GJ, CH, 64, 256)
    route = jnp.stack([destination[:, 0], offset >> 8, offset & 255]).astype(jnp.bfloat16)
    route = jnp.concatenate([route, weight[None]]).reshape(4, GJ, 2, 256).transpose(1, 0, 2, 3)
    route = jnp.broadcast_to(route.reshape(GJ, 1, 8, 256), (GJ, CH, 8, 256))
    outgoing = jnp.concatenate([spectra, route], axis=2).reshape(GJ * CH, 72, 256)
    turned = lax.all_to_all(outgoing, ("gj", "ch"), split_axis=0, concat_axis=0, tiled=True)
    turned = turned.reshape(GJ, CH, 72, 256)
    route = lax.dynamic_index_in_dim(turned[:, :, 64:], ch, 1, keepdims=False)
    route = route.reshape(32, 512)
    volts = turned[:, :, :64].reshape(GJ, CH, 2, 32, 256).transpose(2, 0, 3, 1, 4).reshape(2, 256, SPEC)

    blocks = spread_direct(jnp.concatenate([volts[0], route]), "x")
    re_x = jnp.concatenate([block[:256] for block in blocks])
    route = jnp.concatenate([block[256:] for block in blocks])
    blocks = spread_direct(volts[1], "y")
    im_y = jnp.concatenate(blocks)
    route = jnp.stack(spread_direct(route, "y"))
    re_near, im_near = spread_near(re_x, "y"), spread_near(im_y, "x")

    y, x = gi // 4, gi % 4

    def slot(step):
        step = step & 3
        return jnp.where(step == 0, 0, jnp.where(step == 3, 1, jnp.where(step == 1, 2, 3)))

    slot_of = slot(jnp.arange(16, dtype=jnp.int32) // 4 - y) * 4 + slot(jnp.arange(16, dtype=jnp.int32) % 4 - x)

    route = route.reshape(16, GJ, 4, 512).astype(jnp.float32)
    loads = route[:, :, 3].reshape(ROWS_CH)
    tile = route[:, :, 0].astype(jnp.int32).reshape(ROWS_CH)
    shift = (route[:, :, 1] * 256.0 + route[:, :, 2]).astype(jnp.int32).reshape(ROWS_CH)
    index = jnp.arange(ROWS_CH, dtype=jnp.int32)
    column = (index // 512 % 8) * 2 + index % 2
    row = index // 4096 * 256 + index // 2 % 256
    ahead = ((tile % GJ) // 2 - gj // 2) & 3
    other = (tile % 2) ^ (gj % 2)
    where = jnp.where(ahead == 0, 3, jnp.where(ahead == 3, 2, jnp.where(ahead == 1, 1, 0))) * 2 + other
    keys = column * (1 << 24) + (where * TU + shift) * (1 << 12) + row
    keys = jnp.where(tile // GJ == gi, keys, BIG)
    edges = jnp.arange(2 * GJ + 1, dtype=jnp.int32) * (1 << 24)
    starts = jnp.sum((keys[None, :] < edges[:, None]).astype(jnp.int32), axis=1)
    keys, loads, *_ = lax.optimization_barrier((keys, loads, re_x, im_y))
    keys, loads = lax.sort((keys, loads), num_keys=1, is_stable=False)
    rows, cells = (keys & (N_IN - 1)) * STEPS, ((keys >> 12) & (N_IN - 1)) * 4
    rows, cells, loads, re_near, im_near = lax.optimization_barrier((rows, cells, loads, re_near, im_near))
    volts = spread_far(re_near, im_near)

    keep_far, send_far, keep, send = grid_rows(starts, slot_of, rows, cells, loads, *volts)

    def swap(block):
        return lax.ppermute(block, "gj", [(j, j ^ 1) for j in range(GJ)]).astype(jnp.float32)

    def step(block, by):
        turn = [(z * 2 + c, (z + by) % 4 * 2 + c) for z in range(4) for c in range(2)]
        return lax.ppermute(block.astype(jnp.bfloat16), "gj", turn).astype(jnp.float32)

    half = TU // 2
    across = (keep_far + swap(send_far))[0]
    low, high = step(across[:half], 1), step(across[half:], -1)
    after, before, own = keep + swap(send)
    ahead_high, behind_low = step(after[half:], 1), step(before[:half], -1)
    ahead_low, behind_high = step(after[:half] + low, 1), step(before[half:] + high, -1)
    out = own + jnp.concatenate([ahead_low, ahead_high]) + jnp.concatenate([behind_low, behind_high])
    return out[None, None]


def solution(mesh):
    in_specs = (
        P(("gi", "gj"), "ch", None),
        P(("gi", "gj", "ch"), None),
        P(("gi", "gj", "ch")),
        P(("gi", "gj", "ch")),
    )
    out_specs = P("ch", ("gi", "gj"), None, None)
    return jax.shard_map(shards, mesh=mesh, in_specs=in_specs, out_specs=out_specs, check_vma=False)
```

```python
import math

import jax
import jax.numpy as jnp
from jax import lax
from jax.experimental import pallas as pl
from jax.experimental.pallas import tpu as pltpu
from jax.sharding import PartitionSpec as P

NCHAN = 16
TAPS = 32
SPEC = 512
GI, GJ, CH = 16, 8, 2
N_IN = 4096
TU = 512
TV = 256
LANES = 128
STEPS = 8
SIZES = (256, 384, 512)
CHUNK = SIZES[-1]
UNROLL = 16
ROWS_CH = 65536
BIG = 1 << 29
WINDOW = 8192
SPARE = GJ * TU * 4


def dft_tables():
    sample_index = jnp.arange(TAPS, dtype=jnp.int32)
    channel_index = jnp.arange(NCHAN, dtype=jnp.int32)
    phase = (channel_index[:, None] * sample_index[None, :] % TAPS).astype(jnp.float32) * (
        2.0 * math.pi / TAPS
    )
    return (jnp.cos(phase), -jnp.sin(phase))


def grid_kernel(starts, place, rows, cells, weights, *refs):
    re_all, im_all, outs, scratch = refs[:5], refs[5:10], refs[10:14], refs[14:]
    volts, row_at, cell_at, weight_at, wide, picked, vis, acc, sems, list_sems = scratch
    normalize = 1.0 / (NCHAN * math.sqrt(SPEC))
    copies = []

    def fetch(source, row, count, lane):
        target = volts.at[pl.ds(row, count), pl.ds(lane, SPEC)]
        copy = pltpu.make_async_copy(source, target, sems.at[len(copies)])
        copies.append((copy, row, count, lane))
        copy.start()

    for at, ref in zip((0, 1, 2, 3, 3.5), re_all):
        fetch(ref, int(at * 1024), ref.shape[0], 0)
    for at, ref in zip((0, 1, 2, 3, 3), im_all):
        first = 2 if ref is im_all[4] else 0
        for part in range(ref.shape[0] // 256):
            fetch(ref.at[pl.ds(part * 256, 256)], (first + part) * 1024 + at * 256, 256, SPEC)

    def lists(turn):
        window = pl.ds(pl.multiple_of(turn * WINDOW, WINDOW), WINDOW)
        return [
            pltpu.make_async_copy(source.at[window], target.at[pl.ds(0, WINDOW)], list_sems.at[i])
            for i, (source, target) in enumerate(((rows, row_at), (cells, cell_at), (weights, weight_at)))
        ]

    for copy in lists(0):
        copy.start()

    for i in range(UNROLL):
        row_at[WINDOW + i] = 0
        cell_at[WINDOW + i] = 0
        weight_at[WINDOW + i] = 0.0

    @pl.loop(0, SPARE // 512)
    def _(r):
        acc[pl.ds(pl.multiple_of(r * 512, 512), 512), :] = jnp.zeros((512, LANES), jnp.float32)

    for copy, row, count, lane in copies:
        copy.wait()

        @pl.loop(0, count // 64)
        def _(r, row=row, lane=lane):
            block = volts[pl.ds(pl.multiple_of(row + r * 64, 64), 64), pl.ds(lane, SPEC)].astype(jnp.float32)
            for k in range(4):
                wide[pl.ds((row + r * 64) * STEPS + lane // LANES + k, 64, stride=STEPS), :] = block[
                    :, k * LANES:(k + 1) * LANES
                ]

    def dot(a, b):
        return lax.dot_general(a, b, (((1,), (1,)), ((), ())), preferred_element_type=jnp.float32)

    @pl.loop(0, jnp.maximum((starts[2 * GJ] + WINDOW - 1) // WINDOW, 1))
    def _(turn):
        @pl.when(turn > 0)
        def _():
            for copy in lists(turn):
                copy.start()

        for copy in lists(turn):
            copy.wait()

        @pl.loop(0, 2 * GJ)
        def _(group):
            column, half = group // 2, group % 2
            first = jnp.maximum(starts[group] - turn * WINDOW, 0)
            last = jnp.minimum(starts[group + 1] - turn * WINDOW, WINDOW)

            @pl.loop(0, (jnp.maximum(last - first, 0) + CHUNK - 1) // CHUNK)
            def _(step):
                base = first + step * CHUNK
                count = jnp.minimum(last - base, CHUNK)
                rounds = (count + UNROLL - 1) // UNROLL

                @pl.loop(0, rounds)
                def _(r):
                    at = r * UNROLL
                    for i in range(UNROLL):
                        row = pl.multiple_of(row_at[base + at + i], STEPS)
                        picked[pl.ds(pl.multiple_of((at + i) * STEPS, STEPS), STEPS), :] = wide[pl.ds(row, STEPS), :]

                for low, size in zip((0,) + SIZES, SIZES):

                    @pl.when((count > low) & (count <= size))
                    def _(size=size):
                        blocks = [
                            volts[pl.ds(pl.multiple_of(place[half * 8 + p] * 256 + column * 32, 32), 32), :]
                            for p in range(8)
                        ]
                        columns = jnp.concatenate(blocks, axis=0)
                        pieces = [picked[pl.ds(k, size, stride=STEPS), :].astype(jnp.bfloat16) for k in range(STEPS)]
                        turned = pieces[4:] + [-piece for piece in pieces[:4]]
                        both = jnp.concatenate([jnp.concatenate(pieces, axis=1), jnp.concatenate(turned, axis=1)], axis=0)
                        both = dot(both, columns) * normalize
                        real, imag = both[:size], both[size:]
                        for j, part in enumerate((real[:, :LANES], real[:, LANES:], imag[:, :LANES], imag[:, LANES:])):
                            vis[pl.ds(j, size, stride=4), :] = part.astype(jnp.bfloat16).astype(jnp.float32)

                def add(at, used):
                    where, load, old, new = [], [], [], []
                    for i in range(UNROLL):
                        cell, weight = cell_at[base + at + i], weight_at[base + at + i]
                        if used is not None:
                            cell = jnp.where(i < used, cell, SPARE)
                            weight = jnp.where(i < used, weight, 0.0)
                        where.append(pl.multiple_of(cell, 4))
                        old.append(acc[pl.ds(where[i], 4), :])
                        new.append(weight * vis[pl.ds(pl.multiple_of((at + i) * 4, 4), 4), :])
                    sums = [old[0] + new[0]]
                    for i in range(1, UNROLL):
                        sums.append(jnp.where(where[i] == where[i - 1], sums[-1], old[i]) + new[i])
                    for i in range(UNROLL):
                        acc[pl.ds(where[i], 4), :] = sums[i]

                full = count // UNROLL

                @pl.loop(0, full)
                def _(r):
                    add(r * UNROLL, None)

                @pl.when(count > full * UNROLL)
                def _():
                    add(full * UNROLL, count - full * UNROLL)

    for k in range(4):
        keep, send = outs[:2] if k == 0 else outs[2:]
        to = max(k - 1, 0)
        for j in range(4):
            lanes = slice(j * LANES, (j + 1) * LANES)
            keep[to, :, lanes] = acc[pl.ds(2 * k * TU * 4 + j, TU, stride=4), :]
            send[to, :, lanes] = acc[pl.ds((2 * k + 1) * TU * 4 + j, TU, stride=4), :].astype(jnp.bfloat16)


def grid_rows(starts, place, rows, cells, weights, *volts):
    smem = pl.BlockSpec(memory_space=pltpu.SMEM)
    vmem = pl.BlockSpec(memory_space=pltpu.VMEM)
    return pl.pallas_call(
        grid_kernel,
        out_shape=tuple(
            jax.ShapeDtypeStruct((count, TU, 2 * TV), dtype)
            for count in (1, 3)
            for dtype in (jnp.float32, jnp.bfloat16)
        ),
        in_specs=[smem, smem] + [pl.BlockSpec(memory_space=pl.ANY)] * 13,
        out_specs=(vmem,) * 4,
        scratch_shapes=[
            pltpu.VMEM((N_IN, 2 * SPEC), jnp.bfloat16),
            pltpu.SMEM((WINDOW + UNROLL,), jnp.int32),
            pltpu.SMEM((WINDOW + UNROLL,), jnp.int32),
            pltpu.SMEM((WINDOW + UNROLL,), jnp.float32),
            pltpu.VMEM((N_IN * STEPS, LANES), jnp.float32),
            pltpu.VMEM((CHUNK * STEPS, LANES), jnp.float32),
            pltpu.VMEM((CHUNK * 4, LANES), jnp.float32),
            pltpu.VMEM((SPARE + 8, LANES), jnp.float32),
            pltpu.SemaphoreType.DMA((21,)),
            pltpu.SemaphoreType.DMA((3,)),
        ],
        compiler_params=pltpu.CompilerParams(vmem_limit_bytes=56 * 1024 * 1024),
        cost_estimate=pl.CostEstimate(flops=1 << 33, bytes_accessed=64 << 20, transcendentals=0),
        name="grid_rows",
    )(starts, place, rows, cells, weights, *volts)


def along(axis, step):
    pairs = []
    for y in range(4):
        for x in range(4):
            to = (y + step) % 4 * 4 + x if axis == "y" else y * 4 + (x + step) % 4
            pairs.append((y * 4 + x, to))
    return pairs


def spread_direct(block, axis):
    return [block] + [lax.ppermute(block, "gi", along(axis, step)) for step in (1, -1, 2)]


def spread_near(block, axis):
    return block, lax.ppermute(block, "gi", along(axis, 1)), lax.ppermute(block, "gi", along(axis, -1))


def halves_kernel(*refs):
    for source, target in zip(refs[:4], refs[4:]):
        target[...] = source[...]


def halves(*blocks):
    return pl.pallas_call(
        halves_kernel,
        grid=(2,),
        out_shape=(jax.ShapeDtypeStruct((512, SPEC), jnp.bfloat16),) * 4,
        in_specs=[pl.BlockSpec((256, SPEC), lambda i, at=at: (at + i, 0)) for at in (0, 2, 0, 2)],
        out_specs=(pl.BlockSpec((256, SPEC), lambda i: (i, 0)),) * 4,
        name="halves",
    )(*blocks)


def spread_far(re_near, im_near):
    parts = halves(*re_near[1:], *im_near[1:])
    far = [
        lax.ppermute(part, "gi", along(axis, by))
        for part, axis, by in zip(parts, ("y", "y", "x", "x"), (1, -1, 1, -1))
    ]
    return [*re_near, *far[:2], *im_near, *far[2:]]


def shards(samples, destination, offset, weight):
    gi, gj, ch = lax.axis_index("gi"), lax.axis_index("gj"), lax.axis_index("ch")
    cosine_table, sine_table = dft_tables()
    widened = samples.astype(jnp.float32)
    tables = jnp.stack([cosine_table, sine_table]).reshape(2, CH, GJ, TAPS)
    spectra = jnp.einsum("nst,kblt->lbkns", widened, tables, precision=lax.Precision.HIGHEST)
    spectra = spectra.astype(jnp.bfloat16).reshape(GJ, CH, 64, 256)
    route = jnp.stack([destination[:, 0], offset >> 8, offset & 255]).astype(jnp.bfloat16)
    route = jnp.concatenate([route, weight[None]]).reshape(4, GJ, 2, 256).transpose(1, 0, 2, 3)
    route = jnp.broadcast_to(route.reshape(GJ, 1, 8, 256), (GJ, CH, 8, 256))
    outgoing = jnp.concatenate([spectra, route], axis=2).reshape(GJ * CH, 72, 256)
    turned = lax.all_to_all(outgoing, ("gj", "ch"), split_axis=0, concat_axis=0, tiled=True)
    turned = turned.reshape(GJ, CH, 72, 256)
    route = lax.dynamic_index_in_dim(turned[:, :, 64:], ch, 1, keepdims=False)
    route = route.reshape(32, 512)
    volts = turned[:, :, :64].reshape(GJ, CH, 2, 32, 256).transpose(2, 0, 3, 1, 4).reshape(2, 256, SPEC)

    blocks = spread_direct(jnp.concatenate([volts[0], route]), "x")
    re_x = jnp.concatenate([block[:256] for block in blocks])
    route = jnp.concatenate([block[256:] for block in blocks])
    blocks = spread_direct(volts[1], "y")
    im_y = jnp.concatenate(blocks)
    route = jnp.stack(spread_direct(route, "y"))
    re_near, im_near = spread_near(re_x, "y"), spread_near(im_y, "x")

    y, x = gi // 4, gi % 4

    def slot(step):
        step = step & 3
        return jnp.where(step == 0, 0, jnp.where(step == 3, 1, jnp.where(step == 1, 2, 3)))

    slot_of = slot(jnp.arange(16, dtype=jnp.int32) // 4 - y) * 4 + slot(jnp.arange(16, dtype=jnp.int32) % 4 - x)

    route = route.reshape(16, GJ, 4, 512).astype(jnp.float32)
    loads = route[:, :, 3].reshape(ROWS_CH)
    tile = route[:, :, 0].astype(jnp.int32).reshape(ROWS_CH)
    shift = (route[:, :, 1] * 256.0 + route[:, :, 2]).astype(jnp.int32).reshape(ROWS_CH)
    index = jnp.arange(ROWS_CH, dtype=jnp.int32)
    column = (index // 512 % 8) * 2 + index % 2
    row = index // 4096 * 256 + index // 2 % 256
    ahead = ((tile % GJ) // 2 - gj // 2) & 3
    other = (tile % 2) ^ (gj % 2)
    where = jnp.where(ahead == 0, 3, jnp.where(ahead == 3, 2, jnp.where(ahead == 1, 1, 0))) * 2 + other
    keys = column * (1 << 24) + (where * TU + shift) * (1 << 12) + row
    keys = jnp.where(tile // GJ == gi, keys, BIG)
    edges = jnp.arange(2 * GJ + 1, dtype=jnp.int32) * (1 << 24)
    starts = jnp.sum((keys[None, :] < edges[:, None]).astype(jnp.int32), axis=1)
    keys, loads, *_ = lax.optimization_barrier((keys, loads, re_x, im_y))
    keys, loads = lax.sort((keys, loads), num_keys=1, is_stable=False)
    rows, cells = (keys & (N_IN - 1)) * STEPS, ((keys >> 12) & (N_IN - 1)) * 4
    rows, cells, loads, re_near, im_near = lax.optimization_barrier((rows, cells, loads, re_near, im_near))
    volts = spread_far(re_near, im_near)

    keep_far, send_far, keep, send = grid_rows(starts, slot_of, rows, cells, loads, *volts)

    def swap(block):
        return lax.ppermute(block, "gj", [(j, j ^ 1) for j in range(GJ)]).astype(jnp.float32)

    def step(block, by):
        turn = [(z * 2 + c, (z + by) % 4 * 2 + c) for z in range(4) for c in range(2)]
        return lax.ppermute(block.astype(jnp.bfloat16), "gj", turn).astype(jnp.float32)

    half = TU // 2
    across = (keep_far + swap(send_far))[0]
    low, high = step(across[:half], 1), step(across[half:], -1)
    after, before, own = keep + swap(send)
    ahead_high, behind_low = step(after[half:], 1), step(before[:half], -1)
    ahead_low, behind_high = step(after[:half] + low, 1), step(before[half:] + high, -1)
    out = own + jnp.concatenate([ahead_low, ahead_high]) + jnp.concatenate([behind_low, behind_high])
    return out[None, None]


def solution(mesh):
    in_specs = (
        P(("gi", "gj"), "ch", None),
        P(("gi", "gj", "ch"), None),
        P(("gi", "gj", "ch")),
        P(("gi", "gj", "ch")),
    )
    out_specs = P("ch", ("gi", "gj"), None, None)
    return jax.shard_map(shards, mesh=mesh, in_specs=in_specs, out_specs=out_specs, check_vma=False)
```

```python
import math

import jax
import jax.numpy as jnp
from jax import lax
from jax.experimental import pallas as pl
from jax.experimental.pallas import tpu as pltpu
from jax.sharding import PartitionSpec as P

NCHAN = 16
TAPS = 32
SPEC = 512
GI, GJ, CH = 16, 8, 2
N_IN = 4096
TU = 512
TV = 256
LANES = 128
STEPS = 8
SIZES = (256, 384, 512)
CHUNK = SIZES[-1]
UNROLL = 16
ROWS_CH = 65536
BIG = 1 << 29
WINDOW = 8192
SPARE = GJ * TU * 4


def dft_tables():
    sample_index = jnp.arange(TAPS, dtype=jnp.int32)
    channel_index = jnp.arange(NCHAN, dtype=jnp.int32)
    phase = (channel_index[:, None] * sample_index[None, :] % TAPS).astype(jnp.float32) * (
        2.0 * math.pi / TAPS
    )
    return (jnp.cos(phase), -jnp.sin(phase))


def grid_kernel(starts, place, rows, cells, weights, *refs):
    re_all, im_all, outs, scratch = refs[:5], refs[5:10], refs[10:14], refs[14:]
    volts, row_at, cell_at, weight_at, wide, picked, vis, acc, sems, list_sems = scratch
    normalize = 1.0 / (NCHAN * math.sqrt(SPEC))
    copies = []

    def fetch(source, row, count, lane):
        target = volts.at[pl.ds(row, count), pl.ds(lane, SPEC)]
        copy = pltpu.make_async_copy(source, target, sems.at[len(copies)])
        copies.append((copy, row, count, lane))
        copy.start()

    for at, ref in zip((0, 1, 2, 3, 3.5), re_all):
        fetch(ref, int(at * 1024), ref.shape[0], 0)
    for at, ref in zip((0, 1, 2, 3, 3), im_all):
        first = 2 if ref is im_all[4] else 0
        for part in range(ref.shape[0] // 256):
            fetch(ref.at[pl.ds(part * 256, 256)], (first + part) * 1024 + at * 256, 256, SPEC)

    def lists(turn):
        window = pl.ds(pl.multiple_of(turn * WINDOW, WINDOW), WINDOW)
        return [
            pltpu.make_async_copy(source.at[window], target.at[pl.ds(0, WINDOW)], list_sems.at[i])
            for i, (source, target) in enumerate(((rows, row_at), (cells, cell_at), (weights, weight_at)))
        ]

    for copy in lists(0):
        copy.start()

    for i in range(UNROLL):
        row_at[WINDOW + i] = 0
        cell_at[WINDOW + i] = 0
        weight_at[WINDOW + i] = 0.0

    @pl.loop(0, SPARE // 512)
    def _(r):
        acc[pl.ds(pl.multiple_of(r * 512, 512), 512), :] = jnp.zeros((512, LANES), jnp.float32)

    for copy, row, count, lane in copies:
        copy.wait()

        @pl.loop(0, count // 64)
        def _(r, row=row, lane=lane):
            block = volts[pl.ds(pl.multiple_of(row + r * 64, 64), 64), pl.ds(lane, SPEC)].astype(jnp.float32)
            for k in range(4):
                wide[pl.ds((row + r * 64) * STEPS + lane // LANES + k, 64, stride=STEPS), :] = block[
                    :, k * LANES:(k + 1) * LANES
                ]

    def dot(a, b):
        return lax.dot_general(a, b, (((1,), (1,)), ((), ())), preferred_element_type=jnp.float32)

    @pl.loop(0, jnp.maximum((starts[2 * GJ] + WINDOW - 1) // WINDOW, 1))
    def _(turn):
        @pl.when(turn > 0)
        def _():
            for copy in lists(turn):
                copy.start()

        for copy in lists(turn):
            copy.wait()

        @pl.loop(0, 2 * GJ)
        def _(group):
            column, half = group // 2, group % 2
            first = jnp.maximum(starts[group] - turn * WINDOW, 0)
            last = jnp.minimum(starts[group + 1] - turn * WINDOW, WINDOW)

            @pl.loop(0, (jnp.maximum(last - first, 0) + CHUNK - 1) // CHUNK)
            def _(step):
                base = first + step * CHUNK
                count = jnp.minimum(last - base, CHUNK)
                rounds = (count + UNROLL - 1) // UNROLL

                @pl.loop(0, rounds)
                def _(r):
                    at = r * UNROLL
                    for i in range(UNROLL):
                        row = pl.multiple_of(row_at[base + at + i], STEPS)
                        picked[pl.ds(pl.multiple_of((at + i) * STEPS, STEPS), STEPS), :] = wide[pl.ds(row, STEPS), :]

                for low, size in zip((0,) + SIZES, SIZES):

                    @pl.when((count > low) & (count <= size))
                    def _(size=size):
                        blocks = [
                            volts[pl.ds(pl.multiple_of(place[half * 8 + p] * 256 + column * 32, 32), 32), :]
                            for p in range(8)
                        ]
                        columns = jnp.concatenate(blocks, axis=0)
                        pieces = [picked[pl.ds(k, size, stride=STEPS), :].astype(jnp.bfloat16) for k in range(STEPS)]
                        turned = pieces[4:] + [-piece for piece in pieces[:4]]
                        both = jnp.concatenate([jnp.concatenate(pieces, axis=1), jnp.concatenate(turned, axis=1)], axis=0)
                        both = dot(both, columns) * normalize
                        real, imag = both[:size], both[size:]
                        for j, part in enumerate((real[:, :LANES], real[:, LANES:], imag[:, :LANES], imag[:, LANES:])):
                            vis[pl.ds(j, size, stride=4), :] = part.astype(jnp.bfloat16).astype(jnp.float32)

                def add(at, used):
                    where, load, old, new = [], [], [], []
                    for i in range(UNROLL):
                        cell, weight = cell_at[base + at + i], weight_at[base + at + i]
                        if used is not None:
                            cell = jnp.where(i < used, cell, SPARE)
                            weight = jnp.where(i < used, weight, 0.0)
                        where.append(pl.multiple_of(cell, 4))
                        old.append(acc[pl.ds(where[i], 4), :])
                        new.append(weight * vis[pl.ds(pl.multiple_of((at + i) * 4, 4), 4), :])
                    sums = [old[0] + new[0]]
                    for i in range(1, UNROLL):
                        sums.append(jnp.where(where[i] == where[i - 1], sums[-1], old[i]) + new[i])
                    for i in range(UNROLL):
                        acc[pl.ds(where[i], 4), :] = sums[i]

                full = count // UNROLL

                @pl.loop(0, full)
                def _(r):
                    add(r * UNROLL, None)

                @pl.when(count > full * UNROLL)
                def _():
                    add(full * UNROLL, count - full * UNROLL)

    for k in range(4):
        keep, send = outs[:2] if k == 0 else outs[2:]
        to = max(k - 1, 0)
        for j in range(4):
            lanes = slice(j * LANES, (j + 1) * LANES)
            keep[to, :, lanes] = acc[pl.ds(2 * k * TU * 4 + j, TU, stride=4), :]
            send[to, :, lanes] = acc[pl.ds((2 * k + 1) * TU * 4 + j, TU, stride=4), :].astype(jnp.bfloat16)


def grid_rows(starts, place, rows, cells, weights, *volts):
    smem = pl.BlockSpec(memory_space=pltpu.SMEM)
    vmem = pl.BlockSpec(memory_space=pltpu.VMEM)
    return pl.pallas_call(
        grid_kernel,
        out_shape=tuple(
            jax.ShapeDtypeStruct((count, TU, 2 * TV), dtype)
            for count in (1, 3)
            for dtype in (jnp.float32, jnp.bfloat16)
        ),
        in_specs=[smem, smem] + [pl.BlockSpec(memory_space=pl.ANY)] * 13,
        out_specs=(vmem,) * 4,
        scratch_shapes=[
            pltpu.VMEM((N_IN, 2 * SPEC), jnp.bfloat16),
            pltpu.SMEM((WINDOW + UNROLL,), jnp.int32),
            pltpu.SMEM((WINDOW + UNROLL,), jnp.int32),
            pltpu.SMEM((WINDOW + UNROLL,), jnp.float32),
            pltpu.VMEM((N_IN * STEPS, LANES), jnp.float32),
            pltpu.VMEM((CHUNK * STEPS, LANES), jnp.float32),
            pltpu.VMEM((CHUNK * 4, LANES), jnp.float32),
            pltpu.VMEM((SPARE + 8, LANES), jnp.float32),
            pltpu.SemaphoreType.DMA((21,)),
            pltpu.SemaphoreType.DMA((3,)),
        ],
        compiler_params=pltpu.CompilerParams(vmem_limit_bytes=56 * 1024 * 1024),
        cost_estimate=pl.CostEstimate(flops=1 << 33, bytes_accessed=64 << 20, transcendentals=0),
        name="grid_rows",
    )(starts, place, rows, cells, weights, *volts)


def along(axis, step):
    pairs = []
    for y in range(4):
        for x in range(4):
            to = (y + step) % 4 * 4 + x if axis == "y" else y * 4 + (x + step) % 4
            pairs.append((y * 4 + x, to))
    return pairs


def spread_direct(block, axis):
    return [block] + [lax.ppermute(block, "gi", along(axis, step)) for step in (1, -1, 2)]


def spread_near(block, axis):
    return block, lax.ppermute(block, "gi", along(axis, 1)), lax.ppermute(block, "gi", along(axis, -1))


def halves_kernel(*refs):
    for source, target in zip(refs[:4], refs[4:]):
        target[...] = source[...]


def halves(*blocks):
    return pl.pallas_call(
        halves_kernel,
        grid=(2,),
        out_shape=(jax.ShapeDtypeStruct((512, SPEC), jnp.bfloat16),) * 4,
        in_specs=[pl.BlockSpec((256, SPEC), lambda i, at=at: (at + i, 0)) for at in (0, 2, 0, 2)],
        out_specs=(pl.BlockSpec((256, SPEC), lambda i: (i, 0)),) * 4,
        name="halves",
    )(*blocks)


def spread_far(re_near, im_near):
    parts = halves(*re_near[1:], *im_near[1:])
    far = [
        lax.ppermute(part, "gi", along(axis, by))
        for part, axis, by in zip(parts, ("y", "y", "x", "x"), (1, -1, 1, -1))
    ]
    return [*re_near, *far[:2], *im_near, *far[2:]]


def shards(samples, destination, offset, weight):
    gi, gj, ch = lax.axis_index("gi"), lax.axis_index("gj"), lax.axis_index("ch")
    cosine_table, sine_table = dft_tables()
    widened = samples.astype(jnp.float32)
    tables = jnp.stack([cosine_table, sine_table]).reshape(2, CH, GJ, TAPS)
    spectra = jnp.einsum("nst,kblt->lbkns", widened, tables, precision=lax.Precision.HIGHEST)
    spectra = spectra.astype(jnp.bfloat16).reshape(GJ, CH, 64, 256)
    route = jnp.stack([destination[:, 0], offset >> 8, offset & 255]).astype(jnp.bfloat16)
    route = jnp.concatenate([route, weight[None]]).reshape(4, GJ, 2, 256).transpose(1, 0, 2, 3)
    route = jnp.broadcast_to(route.reshape(GJ, 1, 8, 256), (GJ, CH, 8, 256))
    outgoing = jnp.concatenate([spectra, route], axis=2).reshape(GJ * CH, 72, 256)
    turned = lax.all_to_all(outgoing, ("gj", "ch"), split_axis=0, concat_axis=0, tiled=True)
    turned = turned.reshape(GJ, CH, 72, 256)
    route = lax.dynamic_index_in_dim(turned[:, :, 64:], ch, 1, keepdims=False)
    route = route.reshape(32, 512)
    volts = turned[:, :, :64].reshape(GJ, CH, 2, 32, 256).transpose(2, 0, 3, 1, 4).reshape(2, 256, SPEC)

    blocks = spread_direct(jnp.concatenate([volts[0], route]), "x")
    re_x = jnp.concatenate([block[:256] for block in blocks])
    route = jnp.concatenate([block[256:] for block in blocks])
    blocks = spread_direct(volts[1], "y")
    im_y = jnp.concatenate(blocks)
    route = jnp.stack(spread_direct(route, "y"))
    re_near, im_near = spread_near(re_x, "y"), spread_near(im_y, "x")

    y, x = gi // 4, gi % 4

    def slot(step):
        step = step & 3
        return jnp.where(step == 0, 0, jnp.where(step == 3, 1, jnp.where(step == 1, 2, 3)))

    slot_of = slot(jnp.arange(16, dtype=jnp.int32) // 4 - y) * 4 + slot(jnp.arange(16, dtype=jnp.int32) % 4 - x)

    route = route.reshape(16, GJ, 4, 512).astype(jnp.float32)
    loads = route[:, :, 3].reshape(ROWS_CH)
    tile = route[:, :, 0].astype(jnp.int32).reshape(ROWS_CH)
    shift = (route[:, :, 1] * 256.0 + route[:, :, 2]).astype(jnp.int32).reshape(ROWS_CH)
    index = jnp.arange(ROWS_CH, dtype=jnp.int32)
    column = (index // 512 % 8) * 2 + index % 2
    row = index // 4096 * 256 + index // 2 % 256
    ahead = ((tile % GJ) // 2 - gj // 2) & 3
    other = (tile % 2) ^ (gj % 2)
    where = jnp.where(ahead == 0, 3, jnp.where(ahead == 3, 2, jnp.where(ahead == 1, 1, 0))) * 2 + other
    keys = column * (1 << 24) + (where * TU + shift) * (1 << 12) + row
    keys = jnp.where(tile // GJ == gi, keys, BIG)
    edges = jnp.arange(2 * GJ + 1, dtype=jnp.int32) * (1 << 24)
    starts = jnp.sum((keys[None, :] < edges[:, None]).astype(jnp.int32), axis=1)
    keys, loads, *_ = lax.optimization_barrier((keys, loads, re_x, im_y))
    keys, loads = lax.sort((keys, loads), num_keys=1, is_stable=False)
    rows, cells = (keys & (N_IN - 1)) * STEPS, ((keys >> 12) & (N_IN - 1)) * 4
    rows, cells, loads, re_near, im_near = lax.optimization_barrier((rows, cells, loads, re_near, im_near))
    volts = spread_far(re_near, im_near)

    keep_far, send_far, keep, send = grid_rows(starts, slot_of, rows, cells, loads, *volts)

    def swap(block):
        return lax.ppermute(block, "gj", [(j, j ^ 1) for j in range(GJ)]).astype(jnp.float32)

    def step(block, by):
        turn = [(z * 2 + c, (z + by) % 4 * 2 + c) for z in range(4) for c in range(2)]
        return lax.ppermute(block.astype(jnp.bfloat16), "gj", turn).astype(jnp.float32)

    half = TU // 2
    got_far = swap(send_far)
    send, got_far = lax.optimization_barrier((send, got_far))
    across = (keep_far + got_far)[0]
    low, high = step(across[:half], 1), step(across[half:], -1)
    after, before, own = keep + swap(send)
    ahead_high, behind_low = step(after[half:], 1), step(before[:half], -1)
    low, high, ahead_high, behind_low = lax.optimization_barrier((low, high, ahead_high, behind_low))
    ahead_low, behind_high = step(after[:half] + low, 1), step(before[half:] + high, -1)
    out = own + jnp.concatenate([ahead_low, ahead_high]) + jnp.concatenate([behind_low, behind_high])
    return out[None, None]


def solution(mesh):
    in_specs = (
        P(("gi", "gj"), "ch", None),
        P(("gi", "gj", "ch"), None),
        P(("gi", "gj", "ch")),
        P(("gi", "gj", "ch")),
    )
    out_specs = P("ch", ("gi", "gj"), None, None)
    return jax.shard_map(shards, mesh=mesh, in_specs=in_specs, out_specs=out_specs, check_vma=False)
```

```python
import math

import jax
import jax.numpy as jnp
from jax import lax
from jax.experimental import pallas as pl
from jax.experimental.pallas import tpu as pltpu
from jax.sharding import PartitionSpec as P

NCHAN = 16
TAPS = 32
SPEC = 512
GI, GJ, CH = 16, 8, 2
N_IN = 4096
TU = 512
TV = 256
LANES = 128
STEPS = 8
SIZES = (384,)
CHUNK = SIZES[-1]
UNROLL = 16
ROWS_CH = 65536
BIG = 1 << 29
WINDOW = 8192
SPARE = GJ * TU * 4


def dft_tables():
    sample_index = jnp.arange(TAPS, dtype=jnp.int32)
    channel_index = jnp.arange(NCHAN, dtype=jnp.int32)
    phase = (channel_index[:, None] * sample_index[None, :] % TAPS).astype(jnp.float32) * (
        2.0 * math.pi / TAPS
    )
    return (jnp.cos(phase), -jnp.sin(phase))


def grid_kernel(starts, place, rows, cells, weights, *refs):
    re_all, im_all, outs, scratch = refs[:5], refs[5:10], refs[10:14], refs[14:]
    volts, row_at, cell_at, weight_at, wide, picked, vis, acc, sems, list_sems = scratch
    normalize = 1.0 / (NCHAN * math.sqrt(SPEC))
    copies = []

    def fetch(source, row, count, lane):
        target = volts.at[pl.ds(row, count), pl.ds(lane, SPEC)]
        copy = pltpu.make_async_copy(source, target, sems.at[len(copies)])
        copies.append((copy, row, count, lane))
        copy.start()

    for at, ref in zip((0, 1, 2, 3, 3.5), re_all):
        fetch(ref, int(at * 1024), ref.shape[0], 0)
    for at, ref in zip((0, 1, 2, 3, 3), im_all):
        first = 2 if ref is im_all[4] else 0
        for part in range(ref.shape[0] // 256):
            fetch(ref.at[pl.ds(part * 256, 256)], (first + part) * 1024 + at * 256, 256, SPEC)

    def lists(turn):
        window = pl.ds(pl.multiple_of(turn * WINDOW, WINDOW), WINDOW)
        return [
            pltpu.make_async_copy(source.at[window], target.at[pl.ds(0, WINDOW)], list_sems.at[i])
            for i, (source, target) in enumerate(((rows, row_at), (cells, cell_at), (weights, weight_at)))
        ]

    for copy in lists(0):
        copy.start()

    for i in range(UNROLL):
        row_at[WINDOW + i] = 0
        cell_at[WINDOW + i] = 0
        weight_at[WINDOW + i] = 0.0

    @pl.loop(0, SPARE // 512)
    def _(r):
        acc[pl.ds(pl.multiple_of(r * 512, 512), 512), :] = jnp.zeros((512, LANES), jnp.float32)

    for lane in (0, SPEC):
        for copy, _, _, at in copies:
            if at == lane:
                copy.wait()

        @pl.loop(0, N_IN // 64)
        def _(r, lane=lane):
            block = volts[pl.ds(pl.multiple_of(r * 64, 64), 64), pl.ds(lane, SPEC)].astype(jnp.float32)
            for k in range(4):
                wide[pl.ds(r * 64 * STEPS + lane // LANES + k, 64, stride=STEPS), :] = block[
                    :, k * LANES:(k + 1) * LANES
                ]

    def dot(a, b):
        return lax.dot_general(a, b, (((1,), (1,)), ((), ())), preferred_element_type=jnp.float32)

    @pl.loop(0, jnp.maximum((starts[2 * GJ] + WINDOW - 1) // WINDOW, 1))
    def _(turn):
        @pl.when(turn > 0)
        def _():
            for copy in lists(turn):
                copy.start()

        for copy in lists(turn):
            copy.wait()

        @pl.loop(0, 2 * GJ)
        def _(group):
            column, half = group // 2, group % 2
            first = jnp.maximum(starts[group] - turn * WINDOW, 0)
            last = jnp.minimum(starts[group + 1] - turn * WINDOW, WINDOW)

            @pl.loop(0, (jnp.maximum(last - first, 0) + CHUNK - 1) // CHUNK)
            def _(step):
                base = first + step * CHUNK
                count = jnp.minimum(last - base, CHUNK)
                rounds = (count + UNROLL - 1) // UNROLL

                @pl.loop(0, rounds)
                def _(r):
                    at = r * UNROLL
                    for i in range(UNROLL):
                        row = pl.multiple_of(row_at[base + at + i], STEPS)
                        picked[pl.ds(pl.multiple_of((at + i) * STEPS, STEPS), STEPS), :] = wide[pl.ds(row, STEPS), :]

                for low, size in zip((0,) + SIZES, SIZES):

                    @pl.when((count > low) & (count <= size))
                    def _(size=size):
                        blocks = [
                            volts[pl.ds(pl.multiple_of(place[half * 8 + p] * 256 + column * 32, 32), 32), :]
                            for p in range(8)
                        ]
                        columns = jnp.concatenate(blocks, axis=0)
                        pieces = [picked[pl.ds(k, size, stride=STEPS), :].astype(jnp.bfloat16) for k in range(STEPS)]
                        turned = pieces[4:] + [-piece for piece in pieces[:4]]
                        both = jnp.concatenate([jnp.concatenate(pieces, axis=1), jnp.concatenate(turned, axis=1)], axis=0)
                        both = dot(both, columns) * normalize
                        real, imag = both[:size], both[size:]
                        for j, part in enumerate((real[:, :LANES], real[:, LANES:], imag[:, :LANES], imag[:, LANES:])):
                            vis[pl.ds(j, size, stride=4), :] = part.astype(jnp.bfloat16).astype(jnp.float32)

                def add(at, used):
                    where, load, old, new = [], [], [], []
                    for i in range(UNROLL):
                        cell, weight = cell_at[base + at + i], weight_at[base + at + i]
                        if used is not None:
                            cell = jnp.where(i < used, cell, SPARE)
                            weight = jnp.where(i < used, weight, 0.0)
                        where.append(pl.multiple_of(cell, 4))
                        old.append(acc[pl.ds(where[i], 4), :])
                        new.append(weight * vis[pl.ds(pl.multiple_of((at + i) * 4, 4), 4), :])
                    sums = [old[0] + new[0]]
                    for i in range(1, UNROLL):
                        sums.append(jnp.where(where[i] == where[i - 1], sums[-1], old[i]) + new[i])
                    for i in range(UNROLL):
                        acc[pl.ds(where[i], 4), :] = sums[i]

                full = count // UNROLL

                @pl.loop(0, full)
                def _(r):
                    add(r * UNROLL, None)

                @pl.when(count > full * UNROLL)
                def _():
                    add(full * UNROLL, count - full * UNROLL)

    for k in range(4):
        keep, send = outs[:2] if k == 0 else outs[2:]
        to = max(k - 1, 0)
        for j in range(4):
            lanes = slice(j * LANES, (j + 1) * LANES)
            keep[to, :, lanes] = acc[pl.ds(2 * k * TU * 4 + j, TU, stride=4), :]
            send[to, :, lanes] = acc[pl.ds((2 * k + 1) * TU * 4 + j, TU, stride=4), :].astype(jnp.bfloat16)


def grid_rows(starts, place, rows, cells, weights, *volts):
    smem = pl.BlockSpec(memory_space=pltpu.SMEM)
    vmem = pl.BlockSpec(memory_space=pltpu.VMEM)
    return pl.pallas_call(
        grid_kernel,
        out_shape=tuple(
            jax.ShapeDtypeStruct((count, TU, 2 * TV), dtype)
            for count in (1, 3)
            for dtype in (jnp.float32, jnp.bfloat16)
        ),
        in_specs=[smem, smem] + [pl.BlockSpec(memory_space=pl.ANY)] * 13,
        out_specs=(vmem,) * 4,
        scratch_shapes=[
            pltpu.VMEM((N_IN, 2 * SPEC), jnp.bfloat16),
            pltpu.SMEM((WINDOW + UNROLL,), jnp.int32),
            pltpu.SMEM((WINDOW + UNROLL,), jnp.int32),
            pltpu.SMEM((WINDOW + UNROLL,), jnp.float32),
            pltpu.VMEM((N_IN * STEPS, LANES), jnp.float32),
            pltpu.VMEM((CHUNK * STEPS, LANES), jnp.float32),
            pltpu.VMEM((CHUNK * 4, LANES), jnp.float32),
            pltpu.VMEM((SPARE + 8, LANES), jnp.float32),
            pltpu.SemaphoreType.DMA((21,)),
            pltpu.SemaphoreType.DMA((3,)),
        ],
        compiler_params=pltpu.CompilerParams(vmem_limit_bytes=56 * 1024 * 1024),
        cost_estimate=pl.CostEstimate(flops=1 << 33, bytes_accessed=64 << 20, transcendentals=0),
        name="grid_rows",
    )(starts, place, rows, cells, weights, *volts)


def along(axis, step):
    pairs = []
    for y in range(4):
        for x in range(4):
            to = (y + step) % 4 * 4 + x if axis == "y" else y * 4 + (x + step) % 4
            pairs.append((y * 4 + x, to))
    return pairs


def spread_direct(block, axis):
    return [block] + [lax.ppermute(block, "gi", along(axis, step)) for step in (1, -1, 2)]


def spread_near(block, axis):
    return block, lax.ppermute(block, "gi", along(axis, 1)), lax.ppermute(block, "gi", along(axis, -1))


def halves_kernel(*refs):
    for source, target in zip(refs[:4], refs[4:]):
        target[...] = source[...]


def halves(*blocks):
    return pl.pallas_call(
        halves_kernel,
        grid=(2,),
        out_shape=(jax.ShapeDtypeStruct((512, SPEC), jnp.bfloat16),) * 4,
        in_specs=[pl.BlockSpec((256, SPEC), lambda i, at=at: (at + i, 0)) for at in (0, 2, 0, 2)],
        out_specs=(pl.BlockSpec((256, SPEC), lambda i: (i, 0)),) * 4,
        name="halves",
    )(*blocks)


def spread_far(re_near, im_near):
    parts = halves(*re_near[1:], *im_near[1:])
    far = [
        lax.ppermute(part, "gi", along(axis, by))
        for part, axis, by in zip(parts, ("y", "y", "x", "x"), (1, -1, 1, -1))
    ]
    return [*re_near, *far[:2], *im_near, *far[2:]]


def shards(samples, destination, offset, weight):
    gi, gj, ch = lax.axis_index("gi"), lax.axis_index("gj"), lax.axis_index("ch")
    cosine_table, sine_table = dft_tables()
    widened = samples.astype(jnp.float32)
    tables = jnp.stack([cosine_table, sine_table]).reshape(2, CH, GJ, TAPS)
    spectra = jnp.einsum("nst,kblt->lbkns", widened, tables, precision=lax.Precision.HIGHEST)
    spectra = spectra.astype(jnp.bfloat16).reshape(GJ, CH, 64, 256)
    route = jnp.stack([destination[:, 0], offset >> 8, offset & 255]).astype(jnp.bfloat16)
    route = jnp.concatenate([route, weight[None]]).reshape(4, GJ, 2, 256).transpose(1, 0, 2, 3)
    route = jnp.broadcast_to(route.reshape(GJ, 1, 8, 256), (GJ, CH, 8, 256))
    outgoing = jnp.concatenate([spectra, route], axis=2).reshape(GJ * CH, 72, 256)
    turned = lax.all_to_all(outgoing, ("gj", "ch"), split_axis=0, concat_axis=0, tiled=True)
    turned = turned.reshape(GJ, CH, 72, 256)
    route = lax.dynamic_index_in_dim(turned[:, :, 64:], ch, 1, keepdims=False)
    route = route.reshape(32, 512)
    volts = turned[:, :, :64].reshape(GJ, CH, 2, 32, 256).transpose(2, 0, 3, 1, 4).reshape(2, 256, SPEC)

    blocks = spread_direct(jnp.concatenate([volts[0], route]), "x")
    re_x = jnp.concatenate([block[:256] for block in blocks])
    route = jnp.concatenate([block[256:] for block in blocks])
    blocks = spread_direct(volts[1], "y")
    im_y = jnp.concatenate(blocks)
    route = jnp.stack(spread_direct(route, "y"))
    re_near, im_near = spread_near(re_x, "y"), spread_near(im_y, "x")

    y, x = gi // 4, gi % 4

    def slot(step):
        step = step & 3
        return jnp.where(step == 0, 0, jnp.where(step == 3, 1, jnp.where(step == 1, 2, 3)))

    slot_of = slot(jnp.arange(16, dtype=jnp.int32) // 4 - y) * 4 + slot(jnp.arange(16, dtype=jnp.int32) % 4 - x)

    route = route.reshape(16, GJ, 4, 512).astype(jnp.float32)
    loads = route[:, :, 3].reshape(ROWS_CH)
    tile = route[:, :, 0].astype(jnp.int32).reshape(ROWS_CH)
    shift = (route[:, :, 1] * 256.0 + route[:, :, 2]).astype(jnp.int32).reshape(ROWS_CH)
    index = jnp.arange(ROWS_CH, dtype=jnp.int32)
    column = (index // 512 % 8) * 2 + index % 2
    row = index // 4096 * 256 + index // 2 % 256
    ahead = ((tile % GJ) // 2 - gj // 2) & 3
    other = (tile % 2) ^ (gj % 2)
    where = jnp.where(ahead == 0, 3, jnp.where(ahead == 3, 2, jnp.where(ahead == 1, 1, 0))) * 2 + other
    keys = column * (1 << 24) + (where * TU + shift) * (1 << 12) + row
    keys = jnp.where(tile // GJ == gi, keys, BIG)
    edges = jnp.arange(2 * GJ + 1, dtype=jnp.int32) * (1 << 24)
    starts = jnp.sum((keys[None, :] < edges[:, None]).astype(jnp.int32), axis=1)
    keys, loads, *_ = lax.optimization_barrier((keys, loads, re_x, im_y))
    keys, loads = lax.sort((keys, loads), num_keys=1, is_stable=False)
    rows, cells = (keys & (N_IN - 1)) * STEPS, ((keys >> 12) & (N_IN - 1)) * 4
    rows, cells, loads, re_near, im_near = lax.optimization_barrier((rows, cells, loads, re_near, im_near))
    volts = spread_far(re_near, im_near)

    keep_far, send_far, keep, send = grid_rows(starts, slot_of, rows, cells, loads, *volts)

    def swap(block):
        return lax.ppermute(block, "gj", [(j, j ^ 1) for j in range(GJ)]).astype(jnp.float32)

    def step(block, by):
        turn = [(z * 2 + c, (z + by) % 4 * 2 + c) for z in range(4) for c in range(2)]
        return lax.ppermute(block.astype(jnp.bfloat16), "gj", turn).astype(jnp.float32)

    half = TU // 2
    got_far = swap(send_far)
    send, got_far = lax.optimization_barrier((send, got_far))
    across = (keep_far + got_far)[0]
    low, high = step(across[:half], 1), step(across[half:], -1)
    after, before, own = keep + swap(send)
    ahead_high, behind_low = step(after[half:], 1), step(before[:half], -1)
    low, high, ahead_high, behind_low = lax.optimization_barrier((low, high, ahead_high, behind_low))
    ahead_low, behind_high = step(after[:half] + low, 1), step(before[half:] + high, -1)
    out = own + jnp.concatenate([ahead_low, ahead_high]) + jnp.concatenate([behind_low, behind_high])
    return out[None, None]


def solution(mesh):
    in_specs = (
        P(("gi", "gj"), "ch", None),
        P(("gi", "gj", "ch"), None),
        P(("gi", "gj", "ch")),
        P(("gi", "gj", "ch")),
    )
    out_specs = P("ch", ("gi", "gj"), None, None)
    return jax.shard_map(shards, mesh=mesh, in_specs=in_specs, out_specs=out_specs, check_vma=False)
```
